32 devices in a mesh: seq: 8 (over y, x, core), dp: 4 (over z).
Axes of the slice: x: 2, y: 2, z: 4, core: 2. Of those that a mesh axis runs over, the one named last changes fastest.
Arguments:
- frames: bfloat16 [4, 2048, 1536], P('dp', 'seq'), may hold values from -6 to 6
- lengths: int32 [4], P('dp'), may hold values from 512 to 2048, as said below
- wqkv: bfloat16 [1536, 4608], P(None, 'dp')
- wo: bfloat16 [1536, 1536], replicated, may hold values from -0.15625 to 0.15625
- gain_attn: float32 [1536], replicated, may hold values from 0.1 to 1.9
- gain_conv: float32 [1536], replicated, may hold values from 0.1 to 1.9
- conv_w: float32 [31, 1536], replicated, may hold values from -1 to 1
Outputs:
- block_out: bfloat16 [4, 2048, 1536], P('dp', 'seq')
The draws below stay inside these ranges and needn't reach their ends.
Inputs may be any that keep to these rules, and one draw needn't show every extreme that they name: `lengths`: at least one utterance has all 2048 frames valid.
All inputs are finite; a program needn't handle non-finite values.
Results may differ from the reference program's by a relative error of at most 0.004.
The reference program's roundings to bfloat16 on the way (of `normed`, `qkv`, `probs`, `heads_out` and `conv_in`) count: a program that leaves them out, or rounds other values in their place, can miss the bound.
Values may be sent and summed in bfloat16 or wider, within the bound.
A program may use at most 64 MiB of HBM per device.

```python
import math
import jax
import jax.numpy as jnp
from jax import lax

D = 1536
HEADS = 16
KS = 31
E = 96
HALF = 15
FRAMES = 2048
BATCH = 4


def draw_wqkv(key, part):
    first = jax.random.fold_in(key, 0)
    base = jax.random.normal(first, (D, 3 * D), jnp.float32) / math.sqrt(D)
    return base.astype(jnp.bfloat16)


def draw_lengths(key, part):
    first, second = jax.random.split(key)
    drawn = jax.random.randint(first, (BATCH,), FRAMES // 4, FRAMES + 1)
    chosen = jax.random.randint(second, (), 0, BATCH)
    return jnp.where(jnp.arange(BATCH) == chosen, FRAMES, drawn).astype(jnp.int32)


def block_scale(own_key, dims, cuts, smallest, largest):
    def one(position, parts):
        heights = jax.random.uniform(jax.random.fold_in(jax.random.fold_in(own_key, 6), position), (parts,), jnp.float32, smallest / len(cuts), largest / len(cuts))
        return jnp.repeat(jnp.exp(heights), dims[position] // parts).reshape((-1,) + (1,) * (len(dims) - position - 1))

    factor_of = one(*cuts[0])
    for cut in cuts[1:]:
        factor_of = factor_of * one(*cut)
    return factor_of


def scatter_about(own_key, extent, scale, limit, cuts=(), kind=jnp.bfloat16):
    factor_of = block_scale(own_key, extent, cuts, -0.22, 0.18) if cuts else 1.0
    array = jax.random.normal(own_key, extent, jnp.float32) * scale * factor_of
    return jnp.minimum(jnp.maximum(array, -limit), limit).astype(kind)


def setup_inputs(seed: int = 0) -> dict:
    seeds = jax.random.split(jax.random.key(seed), 8)
    return {
        "frames": scatter_about(seeds[0], (BATCH, FRAMES, D), 1.0, 6.0, ((0, 4), (1, 8))),
        "lengths": draw_lengths(jax.random.fold_in(seeds[7], 71), 0),
        "wqkv": draw_wqkv(jax.random.fold_in(seeds[7], 71), 0),
        "wo": scatter_about(seeds[3], (D, D), D ** -0.5, 0.15625),
        "gain_attn": jnp.clip(1.0 + 0.18 * jax.random.normal(seeds[4], (D,), jnp.float32), 0.1, 1.9),
        "gain_conv": jnp.clip(1.0 + 0.18 * jax.random.normal(seeds[5], (D,), jnp.float32), 0.1, 1.9),
        "conv_w": scatter_about(seeds[6], (KS, D), KS ** -0.5, 1.0, (), jnp.float32),
    }


def layer_norm(values, gain):
    values = values.astype(jnp.float32)
    mean = lax.optimization_barrier(jnp.mean(values, axis=-1, keepdims=True))
    centred = values - mean
    var = lax.optimization_barrier(jnp.mean(centred * centred, axis=-1, keepdims=True))
    return centred * lax.rsqrt(var + 1e-05) * gain

def one_head(head_qkv, length):
    query = head_qkv[:, 0, :].astype(jnp.float32)
    keys = head_qkv[:, 1, :].astype(jnp.float32)
    values = head_qkv[:, 2, :].astype(jnp.float32)
    scores = jnp.dot(query, keys.T) * E ** (-0.5)
    valid = jnp.arange(FRAMES, dtype=jnp.int32) < length
    scores = jnp.where(valid[None, :], scores, -1e+30)
    top = lax.optimization_barrier(jnp.max(scores, axis=-1, keepdims=True))
    weights = jnp.exp(scores - top)
    probs = (weights / lax.optimization_barrier(jnp.sum(weights, axis=-1, keepdims=True))).astype(jnp.bfloat16)
    return jnp.dot(probs.astype(jnp.float32), values).astype(jnp.bfloat16)

def utterance(item, wqkv, wo, gain_attn, gain_conv, conv_w):
    rows, length = item
    normed = layer_norm(rows, gain_attn).astype(jnp.bfloat16)
    qkv = jnp.dot(normed, wqkv, preferred_element_type=jnp.float32).astype(jnp.bfloat16)
    per_head = jnp.transpose(qkv.reshape(FRAMES, HEADS, 3, E), (1, 0, 2, 3))
    outs = lax.map(lambda head_qkv: one_head(head_qkv, length), per_head)
    heads_out = jnp.transpose(outs, (1, 0, 2)).reshape(FRAMES, D)
    mid = rows.astype(jnp.float32) + jnp.dot(heads_out, wo, preferred_element_type=jnp.float32)
    valid = (jnp.arange(FRAMES, dtype=jnp.int32) < length).astype(jnp.float32)
    conv_in = (layer_norm(mid, gain_conv) * valid[:, None]).astype(jnp.bfloat16)
    padded = jnp.pad(conv_in.astype(jnp.float32), ((HALF, HALF), (0, 0)))
    conv = jnp.zeros((FRAMES, D), jnp.float32)
    for tap in range(KS):
        conv = conv + conv_w[tap][None, :] * padded[tap:tap + FRAMES]
    return (mid + conv * jax.nn.sigmoid(conv)).astype(jnp.bfloat16)

def reference(frames, lengths, wqkv, wo, gain_attn, gain_conv, conv_w):
    return lax.map(lambda item: utterance(item, wqkv, wo, gain_attn, gain_conv, conv_w), (frames, lengths))
```

```python
import functools

import jax
import jax.numpy as jnp
from jax import lax
from jax.experimental import pallas as pl
from jax.experimental.pallas import tpu as pltpu
from jax.sharding import PartitionSpec as P

HEADS = 16
HALO = 16
MESH = pl.DeviceIdType.MESH
LIMIT = 48 * 1024 * 1024


def reversed_bits(value, count):
    bits = count.bit_length() - 1
    out = 0
    for i in range(bits):
        out = out + (value // (1 << i)) % 2 * (1 << (bits - 1 - i))
    return out


def head_group(seq, dp, n_seq, n_dp):
    column = seq // (n_seq // n_dp)
    return (reversed_bits(dp, n_dp) + column) % n_dp


def exchange_kernel(
    n_seq, n_dp, frames, gain, w_ref, normed_out, w_out, halo_out, own,
    w_sem, halo_send, halo_recv, local_sem, send_sem, recv_sem, forward_send, forward_recv,
):
    me = lax.axis_index("seq")
    dp = lax.axis_index("dp")
    rows = frames.shape[0]
    half = n_seq // 2
    column = me // (n_seq // n_dp)
    source = head_group(me, dp, n_seq, n_dp)
    target = reversed_bits((dp + n_dp - column) % n_dp, n_dp)
    sibling = me + 1 - 2 * (me % 2)
    left = (me + n_seq - 1) % n_seq
    right = (me + 1) % n_seq
    peers = [(me + 2 * i) % n_seq for i in range(1, half)]

    barrier = pltpu.get_barrier_semaphore()
    for other in peers + [sibling, left, right]:
        pl.semaphore_signal(barrier, inc=1, device_id=(other, dp), device_id_type=MESH)

    @pl.when(target != dp)
    def _():
        pl.semaphore_signal(barrier, inc=1, device_id=(me, source), device_id_type=MESH)
        pl.semaphore_signal(barrier, inc=1, device_id=(me, target), device_id_type=MESH)
        pl.semaphore_wait(barrier, len(peers) + 5)

    @pl.when(target == dp)
    def _():
        pl.semaphore_wait(barrier, len(peers) + 3)

    weights = pltpu.make_async_remote_copy(
        src_ref=w_ref, dst_ref=w_out, send_sem=w_sem.at[0], recv_sem=w_sem.at[1],
        device_id=(me, target), device_id_type=MESH,
    )
    kept = pltpu.make_async_copy(w_ref, w_out, w_sem.at[2])

    @pl.when(target != dp)
    def _():
        weights.start()

    @pl.when(target == dp)
    def _():
        kept.start()

    part = 64

    def norm_part(i, carry):
        where = pl.ds(pl.multiple_of(i * part, part), part)
        values = frames[where, :].astype(jnp.float32)
        mean = jnp.mean(values, axis=-1, keepdims=True)
        centred = values - mean
        var = jnp.mean(centred * centred, axis=-1, keepdims=True)
        own[where, :] = (centred * lax.rsqrt(var + 1e-05) * gain[...]).astype(jnp.bfloat16)
        return carry

    lax.fori_loop(0, rows // part, norm_part, 0)

    copies = []
    for i in range(1, half):
        copies.append(pltpu.make_async_remote_copy(
            src_ref=own, dst_ref=normed_out.at[me], send_sem=send_sem.at[i], recv_sem=recv_sem.at[i],
            device_id=(peers[i - 1], dp), device_id_type=MESH,
        ))
    copies.append(pltpu.make_async_remote_copy(
        src_ref=own, dst_ref=normed_out.at[me], send_sem=send_sem.at[0], recv_sem=recv_sem.at[0],
        device_id=(sibling, dp), device_id_type=MESH,
    ))
    copies.append(pltpu.make_async_remote_copy(
        src_ref=frames.at[pl.ds(0, HALO)], dst_ref=halo_out.at[1],
        send_sem=halo_send.at[0], recv_sem=halo_recv.at[0],
        device_id=(left, dp), device_id_type=MESH,
    ))
    copies.append(pltpu.make_async_remote_copy(
        src_ref=frames.at[pl.ds(rows - HALO, HALO)], dst_ref=halo_out.at[0],
        send_sem=halo_send.at[1], recv_sem=halo_recv.at[1],
        device_id=(right, dp), device_id_type=MESH,
    ))
    for copy in copies:
        copy.start()
    local = pltpu.make_async_copy(own, normed_out.at[me], local_sem)
    local.start()

    forwards = []
    for i in range(1, half):
        origin = (me + n_seq - 2 * i) % n_seq
        copies[i - 1].wait_recv()
        forward = pltpu.make_async_remote_copy(
            src_ref=normed_out.at[origin], dst_ref=normed_out.at[origin],
            send_sem=forward_send.at[i], recv_sem=forward_recv.at[i],
            device_id=(sibling, dp), device_id_type=MESH,
        )
        forward.start()
        forwards.append(forward)
    for copy in copies[half - 1:]:
        copy.wait_recv()
    for forward in forwards:
        forward.wait_recv()
    for copy in copies:
        copy.wait_send()
    for forward in forwards:
        forward.wait_send()
    local.wait()

    @pl.when(target != dp)
    def _():
        weights.wait()

    @pl.when(target == dp)
    def _():
        kept.wait()


def exchange(frames, gain, w, n_seq, n_dp):
    rows, width = frames.shape
    return pl.pallas_call(
        functools.partial(exchange_kernel, n_seq, n_dp),
        out_shape=(
            jax.ShapeDtypeStruct((n_seq, rows, width), jnp.bfloat16),
            jax.ShapeDtypeStruct(w.shape, jnp.bfloat16),
            jax.ShapeDtypeStruct((2, HALO, width), jnp.bfloat16),
        ),
        in_specs=[
            pl.BlockSpec(memory_space=pltpu.VMEM),
            pl.BlockSpec(memory_space=pltpu.VMEM),
            pl.BlockSpec(memory_space=pl.ANY),
        ],
        out_specs=(pl.BlockSpec(memory_space=pl.ANY),) * 3,
        scratch_shapes=[
            pltpu.VMEM((rows, width), jnp.bfloat16),
            pltpu.SemaphoreType.DMA((3,)),
            pltpu.SemaphoreType.DMA((2,)),
            pltpu.SemaphoreType.DMA((2,)),
            pltpu.SemaphoreType.DMA,
            pltpu.SemaphoreType.DMA((n_seq // 2,)),
            pltpu.SemaphoreType.DMA((n_seq // 2,)),
            pltpu.SemaphoreType.DMA((n_seq // 2,)),
            pltpu.SemaphoreType.DMA((n_seq // 2,)),
        ],
        compiler_params=pltpu.CompilerParams(collective_id=0, has_side_effects=True, vmem_limit_bytes=LIMIT),
    )(frames, gain, w)


def attend_kernel(head_size, n_heads, block, length_ref, qkv, out, keys_t, values, queries):
    step = pl.program_id(0)
    total = qkv.shape[0]
    wide = 128
    scale = head_size ** (-0.5) * 1.4426950408889634

    @pl.when(step == 0)
    def _():
        out[0:HALO, :] = jnp.zeros((HALO, out.shape[1]), out.dtype)
        out[total + HALO : total + 2 * HALO, :] = jnp.zeros((HALO, out.shape[1]), out.dtype)
        length = length_ref[0]
        part = 256

        def prepare(i, carry):
            start = pl.multiple_of(i * part, part)
            where = pl.ds(start, part)
            extra = lax.broadcasted_iota(jnp.int32, (part, wide - head_size), 1)
            row = start + lax.broadcasted_iota(jnp.int32, (part, wide - head_size), 0)
            first = extra == 0
            ones = jnp.where(first, 1.0, 0.0).astype(jnp.bfloat16)
            bias = jnp.where(first & (row >= length), -1e30, 0.0).astype(jnp.bfloat16)
            for h in range(n_heads):
                base = h * 3 * head_size
                q = qkv[where, base : base + head_size]
                k = qkv[where, base + head_size : base + 2 * head_size]
                v = qkv[where, base + 2 * head_size : base + 3 * head_size]
                queries[h, where, :] = jnp.concatenate([q, ones], axis=1)
                values[h, where, :] = jnp.concatenate([v, ones], axis=1)
                keys_t[h, :, where] = jnp.concatenate([k, bias], axis=1).T
            return carry

        lax.fori_loop(0, total // part, prepare, 0)

    start = pl.multiple_of(step * block, block)
    where = pl.ds(start, block)
    outs = []
    for h in range(n_heads):
        scores = jnp.dot(queries[h, where, :], keys_t[h], preferred_element_type=jnp.float32)
        top = jnp.max(scores, axis=-1, keepdims=True)
        weights = jnp.exp2((scores - top) * scale).astype(jnp.bfloat16)
        summed = jnp.dot(weights, values[h], preferred_element_type=jnp.float32)
        outs.append((summed[:, :head_size] / summed[:, head_size : head_size + 1]).astype(jnp.bfloat16))
    out[pl.ds(pl.multiple_of(start + HALO, HALO), block), :] = jnp.concatenate(outs, axis=1)


def attend(qkv, length, head_size):
    total, columns = qkv.shape
    n_heads = columns // (3 * head_size)
    block = 256
    return pl.pallas_call(
        functools.partial(attend_kernel, head_size, n_heads, block),
        grid=(total // block,),
        out_shape=jax.ShapeDtypeStruct((total + 2 * HALO, n_heads * head_size), jnp.bfloat16),
        in_specs=[
            pl.BlockSpec(memory_space=pltpu.SMEM),
            pl.BlockSpec((total, columns), lambda i: (0, 0)),
        ],
        out_specs=pl.BlockSpec((total + 2 * HALO, n_heads * head_size), lambda i: (0, 0)),
        scratch_shapes=[
            pltpu.VMEM((n_heads, 128, total), jnp.bfloat16),
            pltpu.VMEM((n_heads, total, 128), jnp.bfloat16),
            pltpu.VMEM((n_heads, total, 128), jnp.bfloat16),
        ],
        compiler_params=pltpu.CompilerParams(vmem_limit_bytes=LIMIT),
    )(length, qkv)


def return_kernel(n_seq, count, attended, parts, local_sem, send_sem, recv_sem):
    me = lax.axis_index("seq")
    dp = lax.axis_index("dp")
    others = [(me + i) % n_seq for i in range(1, n_seq)]
    barrier = pltpu.get_barrier_semaphore()
    for other in others:
        pl.semaphore_signal(barrier, inc=1, device_id=(other, dp), device_id_type=MESH)
    pl.semaphore_wait(barrier, n_seq - 1)

    def rows_of(owner):
        return attended.at[pl.ds(pl.multiple_of(owner * count, count), count + 2 * HALO)]

    copies = []
    for i, other in enumerate(others):
        copy = pltpu.make_async_remote_copy(
            src_ref=rows_of(other), dst_ref=parts.at[me], send_sem=send_sem.at[i], recv_sem=recv_sem.at[i],
            device_id=(other, dp), device_id_type=MESH,
        )
        copy.start()
        copies.append(copy)
    local = pltpu.make_async_copy(rows_of(me), parts.at[me], local_sem)
    local.start()
    for copy in copies:
        copy.wait()
    local.wait()


def send_back(attended, n_seq, count):
    return pl.pallas_call(
        functools.partial(return_kernel, n_seq, count),
        out_shape=jax.ShapeDtypeStruct((n_seq, count + 2 * HALO, attended.shape[1]), jnp.bfloat16),
        in_specs=[pl.BlockSpec(memory_space=pl.ANY)],
        out_specs=pl.BlockSpec(memory_space=pl.ANY),
        scratch_shapes=[
            pltpu.SemaphoreType.DMA,
            pltpu.SemaphoreType.DMA((n_seq - 1,)),
            pltpu.SemaphoreType.DMA((n_seq - 1,)),
        ],
        compiler_params=pltpu.CompilerParams(collective_id=1, has_side_effects=True, vmem_limit_bytes=LIMIT),
    )(attended)


def finish_kernel(n_seq, n_dp, length_ref, parts, frames, halo, wo, gain, conv_w, out, mid, padded):
    me = lax.axis_index("seq")
    dp = lax.axis_index("dp")
    count, width = frames.shape
    tall = count + 2 * HALO
    share = n_seq // n_dp
    depth = parts.shape[2]
    taps = conv_w.shape[0]
    reach = (taps - 1) // 2
    cut = 512

    for c in range(width // cut):
        columns = slice(c * cut, (c + 1) * cut)
        total = jnp.concatenate(
            [halo[0, :, columns], frames[:, columns], halo[1, :, columns]], axis=0
        ).astype(jnp.float32)
        for s in range(n_seq):
            slot = head_group(s, dp, n_seq, n_dp) * share + s % share
            rows = pl.ds(pl.multiple_of(slot * depth, depth), depth)
            total = total + jnp.dot(parts[s], wo[rows, columns], preferred_element_type=jnp.float32)
        mid[:, columns] = total

    part = 32

    def norm_part(i, carry):
        start = pl.multiple_of(i * part, part)
        where = pl.ds(start, part)
        values = mid[where, :]
        mean = jnp.mean(values, axis=-1, keepdims=True)
        centred = values - mean
        var = jnp.mean(centred * centred, axis=-1, keepdims=True)
        position = me * count - HALO + start + lax.broadcasted_iota(jnp.int32, (part, 1), 0)
        valid = (position >= 0) & (position < length_ref[0])
        normed = centred * lax.rsqrt(var + 1e-05) * gain[...]
        padded[where, :] = jnp.where(valid, normed, 0.0).astype(jnp.bfloat16).astype(jnp.float32)
        return carry

    lax.fori_loop(0, tall // part, norm_part, 0)

    lanes = 128

    def conv_part(c, carry):
        columns = pl.ds(pl.multiple_of(c * lanes, lanes), lanes)
        for half in range(count // 128):
            base = half * 128
            conv = jnp.zeros((128, lanes), jnp.float32)
            for tap in range(taps):
                first = base + HALO - reach + tap
                conv = conv + conv_w[tap : tap + 1, columns] * padded[first : first + 128, columns]
            result = mid[base + HALO : base + HALO + 128, columns] + conv * jax.nn.sigmoid(conv)
            out[base : base + 128, columns] = result.astype(jnp.bfloat16)
        return carry

    lax.fori_loop(0, width // lanes, conv_part, 0)


def finish(length, parts, frames, halo, wo, gain, conv_w, n_seq, n_dp):
    count, width = frames.shape
    return pl.pallas_call(
        functools.partial(finish_kernel, n_seq, n_dp),
        out_shape=jax.ShapeDtypeStruct((count, width), jnp.bfloat16),
        in_specs=[pl.BlockSpec(memory_space=pltpu.SMEM)] + [pl.BlockSpec(memory_space=pltpu.VMEM)] * 6,
        out_specs=pl.BlockSpec(memory_space=pltpu.VMEM),
        scratch_shapes=[
            pltpu.VMEM((count + 2 * HALO, width), jnp.float32),
            pltpu.VMEM((count + 2 * HALO, width), jnp.float32),
        ],
        compiler_params=pltpu.CompilerParams(vmem_limit_bytes=LIMIT),
    )(length, parts, frames, halo, wo, gain, conv_w)


def body(n_seq, n_dp, frames, lengths, wqkv, wo, gain_attn, gain_conv, conv_w):
    rows = frames[0]
    count, width = rows.shape
    head_size = width // HEADS
    share = n_seq // n_dp
    columns = wqkv.shape[1] // share
    seq = lax.axis_index("seq")
    w = lax.dynamic_slice_in_dim(wqkv, seq % share * columns, columns, axis=1)
    normed, w, halo = exchange(rows, gain_attn[None], w, n_seq, n_dp)
    qkv = jnp.dot(
        normed.reshape(n_seq * count, width), w, preferred_element_type=jnp.float32
    ).astype(jnp.bfloat16)
    attended = attend(qkv, lengths, head_size)
    parts = send_back(attended, n_seq, count)
    return finish(lengths, parts, rows, halo, wo, gain_conv[None], conv_w, n_seq, n_dp)[None]


def solution(mesh):
    return jax.shard_map(
        functools.partial(body, mesh.shape["seq"], mesh.shape["dp"]),
        mesh=mesh,
        in_specs=(P("dp", "seq", None), P("dp"), P(None, "dp"), P(), P(), P(), P()),
        out_specs=P("dp", "seq", None),
        check_vma=False,
    )
```

```python
import functools

import jax
import jax.numpy as jnp
from jax import lax
from jax.experimental import pallas as pl
from jax.experimental.pallas import tpu as pltpu
from jax.sharding import PartitionSpec as P

HEADS = 16
HALO = 16
MESH = pl.DeviceIdType.MESH
LIMIT = 48 * 1024 * 1024


def reversed_bits(value, count):
    bits = count.bit_length() - 1
    out = 0
    for i in range(bits):
        out = out + (value // (1 << i)) % 2 * (1 << (bits - 1 - i))
    return out


def head_group(seq, dp, n_seq, n_dp):
    column = seq // (n_seq // n_dp)
    return (reversed_bits(dp, n_dp) + column) % n_dp


def attention_kernel(
    n_seq, n_dp, head_size, length_ref, frames_ref, gain, w_ref, parts, halo_out,
    frames, normed, w, acc, keys_t, values, queries, attended,
    frame_sem, w_send, w_recv, halo_send, halo_recv,
    send_sem, recv_sem, forward_send, forward_recv, back_send, back_recv,
):
    me = lax.axis_index("seq")
    dp = lax.axis_index("dp")
    rows, width = frames.shape
    total = n_seq * rows
    half = n_seq // 2
    column = me // (n_seq // n_dp)
    source = head_group(me, dp, n_seq, n_dp)
    target = reversed_bits((dp + n_dp - column) % n_dp, n_dp)
    sibling = me + 1 - 2 * (me % 2)
    left = (me + n_seq - 1) % n_seq
    right = (me + 1) % n_seq
    peers = [(me + 2 * i) % n_seq for i in range(1, half)]
    n_heads = w.shape[1] // (3 * head_size)
    wide = 128

    load = pltpu.make_async_copy(frames_ref, frames, frame_sem)
    load.start()
    barrier = pltpu.get_barrier_semaphore()
    for i in range(1, n_seq):
        pl.semaphore_signal(barrier, inc=1, device_id=((me + i) % n_seq, dp), device_id_type=MESH)

    @pl.when(target != dp)
    def _():
        pl.semaphore_signal(barrier, inc=1, device_id=(me, source), device_id_type=MESH)
        pl.semaphore_signal(barrier, inc=1, device_id=(me, target), device_id_type=MESH)
        pl.semaphore_wait(barrier, n_seq + 1)

    @pl.when(target == dp)
    def _():
        pl.semaphore_wait(barrier, n_seq - 1)

    pieces = 3
    deep = width // pieces

    def weights(c):
        where = pl.ds(c * deep, deep)
        return pltpu.make_async_remote_copy(
            src_ref=w_ref.at[where], dst_ref=w.at[where], send_sem=w_send.at[c], recv_sem=w_recv.at[c],
            device_id=(me, target), device_id_type=MESH,
        )

    def kept(c):
        where = pl.ds(c * deep, deep)
        return pltpu.make_async_copy(w_ref.at[where], w.at[where], w_recv.at[c])

    @pl.when(target != dp)
    def _():
        for c in range(pieces):
            weights(c).start()

    @pl.when(target == dp)
    def _():
        for c in range(pieces):
            kept(c).start()

    load.wait()
    part = 64

    def norm_part(i, carry):
        where = pl.ds(pl.multiple_of(i * part, part), part)
        numbers = frames[where, :].astype(jnp.float32)
        mean = jnp.mean(numbers, axis=-1, keepdims=True)
        centred = numbers - mean
        var = jnp.mean(centred * centred, axis=-1, keepdims=True)
        normed[me, where, :] = (centred * lax.rsqrt(var + 1e-05) * gain[...]).astype(jnp.bfloat16)
        return carry

    lax.fori_loop(0, rows // part, norm_part, 0)

    copies = []
    for i in range(half):
        copies.append(pltpu.make_async_remote_copy(
            src_ref=normed.at[me], dst_ref=normed.at[me], send_sem=send_sem.at[i], recv_sem=recv_sem.at[i],
            device_id=(peers[i - 1] if i else sibling, dp), device_id_type=MESH,
        ))
    copies.append(pltpu.make_async_remote_copy(
        src_ref=frames.at[pl.ds(0, HALO)], dst_ref=halo_out.at[1],
        send_sem=halo_send.at[0], recv_sem=halo_recv.at[0],
        device_id=(left, dp), device_id_type=MESH,
    ))
    copies.append(pltpu.make_async_remote_copy(
        src_ref=frames.at[pl.ds(rows - HALO, HALO)], dst_ref=halo_out.at[0],
        send_sem=halo_send.at[1], recv_sem=halo_recv.at[1],
        device_id=(right, dp), device_id_type=MESH,
    ))
    for copy in copies[1:] + copies[:1]:
        copy.start()

    forwards = []
    for i in range(1, half):
        origin = (me + n_seq - 2 * i) % n_seq
        copies[i].wait_recv()
        forward = pltpu.make_async_remote_copy(
            src_ref=normed.at[origin], dst_ref=normed.at[origin],
            send_sem=forward_send.at[i], recv_sem=forward_recv.at[i],
            device_id=(sibling, dp), device_id_type=MESH,
        )
        forward.start()
        forwards.append(forward)
    for copy in copies[:1] + copies[half:]:
        copy.wait_recv()
    for forward in forwards:
        forward.wait_recv()

    for c in range(pieces):
        @pl.when(target != dp)
        def _():
            weights(c).wait()

        @pl.when(target == dp)
        def _():
            kept(c).wait()

        depth = slice(c * deep, (c + 1) * deep)

        def product(s, carry):
            where = pl.ds(pl.multiple_of(s * rows, rows), rows)
            term = jnp.dot(normed[s, :, depth], w[depth, :], preferred_element_type=jnp.float32)
            if c:
                term = acc[where, :] + term
            if c < pieces - 1:
                acc[where, :] = term
                return carry
            qkv = term.astype(jnp.bfloat16)
            extra = lax.broadcasted_iota(jnp.int32, (rows, wide - head_size), 1)
            row = s * rows + lax.broadcasted_iota(jnp.int32, (rows, wide - head_size), 0)
            first = extra == 0
            ones = jnp.where(first, 1.0, 0.0).astype(jnp.bfloat16)
            bias = jnp.where(first & (row >= length_ref[0]), -1e30, 0.0).astype(jnp.bfloat16)
            for h in range(n_heads):
                q, k, v = (
                    qkv[:, (3 * h + p) * head_size : (3 * h + p + 1) * head_size] for p in range(3)
                )
                queries[h, where, :] = jnp.concatenate([q, ones], axis=1)
                values[h, where, :] = jnp.concatenate([v, ones], axis=1)
                keys_t[h, :, where] = jnp.concatenate([k, bias], axis=1).T
            return carry

        lax.fori_loop(0, n_seq, product, 0)

    scale = head_size ** (-0.5) * 1.4426950408889634
    places = [(0, rows, HALO), (rows - HALO, HALO, 0), (0, HALO, rows + HALO)]

    def back(kind, offset):
        dest = (me + offset) % n_seq
        block = (dest + n_seq - (0, 1, n_seq - 1)[kind]) % n_seq
        first, size, at = places[kind]
        src = attended.at[pl.ds(pl.multiple_of(block * rows + first, HALO), size)]
        dst = parts.at[me, pl.ds(at, size)]
        remote = pltpu.make_async_remote_copy(
            src_ref=src, dst_ref=dst, send_sem=back_send.at[kind, offset], recv_sem=back_recv.at[kind, offset],
            device_id=(dest, dp), device_id_type=MESH,
        )
        return remote, pltpu.make_async_copy(src, dst, back_recv.at[kind, offset])

    def attend(i, carry):
        block = (me + 1 + i) % n_seq
        where = pl.ds(pl.multiple_of(block * rows, rows), rows)
        outs = []
        for h in range(n_heads):
            scores = jnp.dot(queries[h, where, :], keys_t[h], preferred_element_type=jnp.float32)
            top = jnp.max(scores, axis=-1, keepdims=True)
            weight = jnp.exp2((scores - top) * scale).astype(jnp.bfloat16)
            summed = jnp.dot(weight, values[h], preferred_element_type=jnp.float32)
            outs.append((summed[:, :head_size] / summed[:, head_size : head_size + 1]).astype(jnp.bfloat16))
        attended[where, :] = jnp.concatenate(outs, axis=1)
        for kind, shift in enumerate((0, 1, n_seq - 1)):
            offset = (i + 1 + shift) % n_seq

            @pl.when(offset != 0)
            def _():
                back(kind, offset)[0].start()

            @pl.when(offset == 0)
            def _():
                back(kind, offset)[1].start()

        return carry

    lax.fori_loop(0, n_seq, attend, 0)

    for kind in range(3):
        back(kind, 0)[1].wait()
        for offset in range(1, n_seq):
            back(kind, offset)[0].wait()
    for copy in copies + forwards:
        copy.wait_send()


def attention(length, frames, gain, w, n_seq, n_dp, head_size):
    rows, width = frames.shape
    total = n_seq * rows
    n_heads = w.shape[1] // (3 * head_size)
    half = n_seq // 2
    dma = pltpu.SemaphoreType.DMA
    return pl.pallas_call(
        functools.partial(attention_kernel, n_seq, n_dp, head_size),
        out_shape=(
            jax.ShapeDtypeStruct((n_seq, rows + 2 * HALO, n_heads * head_size), jnp.bfloat16),
            jax.ShapeDtypeStruct((2, HALO, width), jnp.bfloat16),
        ),
        in_specs=[
            pl.BlockSpec(memory_space=pltpu.SMEM),
            pl.BlockSpec(memory_space=pl.ANY),
            pl.BlockSpec(memory_space=pltpu.VMEM),
            pl.BlockSpec(memory_space=pl.ANY),
        ],
        out_specs=(pl.BlockSpec(memory_space=pl.ANY),) * 2,
        scratch_shapes=[
            pltpu.VMEM((rows, width), jnp.bfloat16),
            pltpu.VMEM((n_seq, rows, width), jnp.bfloat16),
            pltpu.VMEM(w.shape, jnp.bfloat16),
            pltpu.VMEM((total, w.shape[1]), jnp.float32),
            pltpu.VMEM((n_heads, 128, total), jnp.bfloat16),
            pltpu.VMEM((n_heads, total, 128), jnp.bfloat16),
            pltpu.VMEM((n_heads, total, 128), jnp.bfloat16),
            pltpu.VMEM((total, n_heads * head_size), jnp.bfloat16),
            dma, dma((3,)), dma((3,)), dma((2,)), dma((2,)),
            dma((half,)), dma((half,)), dma((half,)), dma((half,)),
            dma((3, n_seq)), dma((3, n_seq)),
        ],
        compiler_params=pltpu.CompilerParams(collective_id=0, has_side_effects=True, vmem_limit_bytes=LIMIT),
    )(length, frames, gain, w)


def finish_kernel(n_seq, n_dp, length_ref, parts, frames, halo, wo, gain, conv_w, out, mid, padded):
    me = lax.axis_index("seq")
    dp = lax.axis_index("dp")
    count, width = frames.shape
    tall = count + 2 * HALO
    share = n_seq // n_dp
    depth = parts.shape[2]
    taps = conv_w.shape[0]
    reach = (taps - 1) // 2
    cut = 512

    for c in range(width // cut):
        columns = slice(c * cut, (c + 1) * cut)
        total = jnp.concatenate(
            [halo[0, :, columns], frames[:, columns], halo[1, :, columns]], axis=0
        ).astype(jnp.float32)
        for s in range(n_seq):
            slot = head_group(s, dp, n_seq, n_dp) * share + s % share
            rows = pl.ds(pl.multiple_of(slot * depth, depth), depth)
            total = total + jnp.dot(parts[s], wo[rows, columns], preferred_element_type=jnp.float32)
        mid[:, columns] = total

    part = 32

    def norm_part(i, carry):
        start = pl.multiple_of(i * part, part)
        where = pl.ds(start, part)
        values = mid[where, :]
        mean = jnp.mean(values, axis=-1, keepdims=True)
        centred = values - mean
        var = jnp.mean(centred * centred, axis=-1, keepdims=True)
        position = me * count - HALO + start + lax.broadcasted_iota(jnp.int32, (part, 1), 0)
        valid = (position >= 0) & (position < length_ref[0])
        normed = centred * lax.rsqrt(var + 1e-05) * gain[...]
        padded[where, :] = jnp.where(valid, normed, 0.0).astype(jnp.bfloat16).astype(jnp.float32)
        return carry

    lax.fori_loop(0, tall // part, norm_part, 0)

    lanes = 128

    def conv_part(c, carry):
        columns = pl.ds(pl.multiple_of(c * lanes, lanes), lanes)
        for half in range(count // 128):
            base = half * 128
            conv = jnp.zeros((128, lanes), jnp.float32)
            for turn in range(8):
                group = [tap for tap in range(taps) if (tap + HALO - reach) % 8 == turn]
                if not group:
                    continue
                low = (group[0] + HALO - reach) // 8 * 8
                high = (group[-1] + HALO - reach) // 8 * 8
                moved = padded[base + low + turn : base + high + turn + 128, columns]
                for tap in group:
                    first = (tap + HALO - reach) // 8 * 8 - low
                    conv = conv + conv_w[tap : tap + 1, columns] * moved[first : first + 128]
            result = mid[base + HALO : base + HALO + 128, columns] + conv * jax.nn.sigmoid(conv)
            out[base : base + 128, columns] = result.astype(jnp.bfloat16)
        return carry

    lax.fori_loop(0, width // lanes, conv_part, 0)


def finish(length, parts, frames, halo, wo, gain, conv_w, n_seq, n_dp):
    count, width = frames.shape
    return pl.pallas_call(
        functools.partial(finish_kernel, n_seq, n_dp),
        out_shape=jax.ShapeDtypeStruct((count, width), jnp.bfloat16),
        in_specs=[pl.BlockSpec(memory_space=pltpu.SMEM)] + [pl.BlockSpec(memory_space=pltpu.VMEM)] * 6,
        out_specs=pl.BlockSpec(memory_space=pltpu.VMEM),
        scratch_shapes=[
            pltpu.VMEM((count + 2 * HALO, width), jnp.float32),
            pltpu.VMEM((count + 2 * HALO, width), jnp.float32),
        ],
        compiler_params=pltpu.CompilerParams(vmem_limit_bytes=LIMIT),
    )(length, parts, frames, halo, wo, gain, conv_w)


def body(n_seq, n_dp, frames, lengths, wqkv, wo, gain_attn, gain_conv, conv_w):
    rows = frames[0]
    count, width = rows.shape
    head_size = width // HEADS
    share = n_seq // n_dp
    columns = wqkv.shape[1] // share
    seq = lax.axis_index("seq")
    w = lax.dynamic_slice_in_dim(wqkv, seq % share * columns, columns, axis=1)
    parts, halo = attention(lengths, rows, gain_attn[None], w, n_seq, n_dp, head_size)
    return finish(lengths, parts, rows, halo, wo, gain_conv[None], conv_w, n_seq, n_dp)[None]


def solution(mesh):
    return jax.shard_map(
        functools.partial(body, mesh.shape["seq"], mesh.shape["dp"]),
        mesh=mesh,
        in_specs=(P("dp", "seq", None), P("dp"), P(None, "dp"), P(), P(), P(), P()),
        out_specs=P("dp", "seq", None),
        check_vma=False,
    )
```

```python
import functools

import jax
import jax.numpy as jnp
from jax import lax
from jax.experimental import pallas as pl
from jax.experimental.pallas import tpu as pltpu
from jax.sharding import PartitionSpec as P

HEADS = 16
HALO = 16
MESH = pl.DeviceIdType.MESH


def reversed_bits(value, count):
    bits = count.bit_length() - 1
    out = 0
    for i in range(bits):
        out = out + (value // (1 << i)) % 2 * (1 << (bits - 1 - i))
    return out


def head_group(seq, dp, n_seq, n_dp):
    column = seq // (n_seq // n_dp)
    return (reversed_bits(dp, n_dp) + column) % n_dp


def attention_kernel(
    n_seq, n_dp, head_size, pieces, length_ref, frames_ref, gain, gain_conv, conv_w, w_ref, wo_ref, out,
    parts, halo_out, wo_out, mid, padded, heads,
    frames, normed, w_full, keys_t, values, queries, attended,
    frame_sem, w_sem, wo_sem, w_send, w_recv, halo_send, halo_recv,
    send_sem, recv_sem, forward_send, forward_recv, back_send, back_recv, *w_parts,
):
    count = len(pieces)
    w_own, w_got = w_parts[:count], w_parts[count:]
    me = lax.axis_index("seq")
    dp = lax.axis_index("dp")
    rows, width = frames.shape
    total = n_seq * rows
    half = n_seq // 2
    column = me // (n_seq // n_dp)
    source = head_group(me, dp, n_seq, n_dp)
    target = reversed_bits((dp + n_dp - column) % n_dp, n_dp)
    sibling = me + 1 - 2 * (me % 2)
    left = (me + n_seq - 1) % n_seq
    right = (me + 1) % n_seq
    peers = [(me + 2 * i) % n_seq for i in range(1, half)]
    n_heads = attended.shape[0]
    share = n_seq // n_dp
    wide = 128

    w_load = pltpu.make_async_copy(w_ref, w_full, w_sem)
    w_load.start()
    load = pltpu.make_async_copy(frames_ref, frames, frame_sem)
    load.start()
    barrier = pltpu.get_barrier_semaphore()
    for i in range(1, n_seq):
        pl.semaphore_signal(barrier, inc=1, device_id=((me + i) % n_seq, dp), device_id_type=MESH)

    @pl.when(target != dp)
    def _():
        pl.semaphore_signal(barrier, inc=1, device_id=(me, source), device_id_type=MESH)
        pl.semaphore_signal(barrier, inc=1, device_id=(me, target), device_id_type=MESH)
        pl.semaphore_wait(barrier, n_seq + 1)

    @pl.when(target == dp)
    def _():
        pl.semaphore_wait(barrier, n_seq - 1)

    def weights(c):
        return pltpu.make_async_remote_copy(
            src_ref=w_own[c], dst_ref=w_got[c], send_sem=w_send.at[c], recv_sem=w_recv.at[c],
            device_id=(me, target), device_id_type=MESH,
        )

    def kept(c):
        return pltpu.make_async_copy(w_own[c], w_got[c], w_recv.at[c])

    w_load.wait()
    for c in range(count):
        for j in range(share):
            @pl.when(me % share == j)
            def _():
                def cut(i, carry):
                    where = pl.ds(pl.multiple_of(i * 256, 256), 256)
                    w_own[c][where, :] = jnp.concatenate(
                        [
                            w_full[where, ((j * n_heads + h) * 3 + p) * head_size : ((j * n_heads + h) * 3 + p + 1) * head_size]
                            for h, p in pieces[c]
                        ],
                        axis=1,
                    )
                    return carry

                lax.fori_loop(0, width // 256, cut, 0)

        @pl.when(target != dp)
        def _():
            weights(c).start()

        @pl.when(target == dp)
        def _():
            kept(c).start()

    load.wait()
    part = 64

    def norm_part(i, carry):
        where = pl.ds(pl.multiple_of(i * part, part), part)
        numbers = frames[where, :].astype(jnp.float32)
        mean = jnp.mean(numbers, axis=-1, keepdims=True)
        centred = numbers - mean
        var = jnp.mean(centred * centred, axis=-1, keepdims=True)
        normed[me, where, :] = (centred * lax.rsqrt(var + 1e-05) * gain[...]).astype(jnp.bfloat16)
        return carry

    lax.fori_loop(0, rows // part, norm_part, 0)

    copies = []
    for i in range(half):
        copies.append(pltpu.make_async_remote_copy(
            src_ref=normed.at[me], dst_ref=normed.at[me], send_sem=send_sem.at[i], recv_sem=recv_sem.at[i],
            device_id=(peers[i - 1] if i else sibling, dp), device_id_type=MESH,
        ))
    copies.append(pltpu.make_async_remote_copy(
        src_ref=frames.at[pl.ds(0, HALO)], dst_ref=halo_out.at[1],
        send_sem=halo_send.at[0], recv_sem=halo_recv.at[0],
        device_id=(left, dp), device_id_type=MESH,
    ))
    copies.append(pltpu.make_async_remote_copy(
        src_ref=frames.at[pl.ds(rows - HALO, HALO)], dst_ref=halo_out.at[0],
        send_sem=halo_send.at[1], recv_sem=halo_recv.at[1],
        device_id=(right, dp), device_id_type=MESH,
    ))
    for copy in copies[1:] + copies[:1]:
        copy.start()

    depth = n_heads * head_size
    reorders = []
    for i in range(n_seq):
        slot = head_group(i, dp, n_seq, n_dp) * share + i % share
        reorder = pltpu.make_async_copy(
            wo_ref.at[pl.ds(pl.multiple_of(slot * depth, depth), depth)],
            wo_out.at[pl.ds(i * depth, depth)],
            wo_sem.at[i],
        )
        reorder.start()
        reorders.append(reorder)

    forwards = []
    for i in range(1, half):
        origin = (me + n_seq - 2 * i) % n_seq
        copies[i].wait_recv()
        forward = pltpu.make_async_remote_copy(
            src_ref=normed.at[origin], dst_ref=normed.at[origin],
            send_sem=forward_send.at[i], recv_sem=forward_recv.at[i],
            device_id=(sibling, dp), device_id_type=MESH,
        )
        forward.start()
        forwards.append(forward)
    for copy in copies[:1] + copies[half:]:
        copy.wait_recv()
    for forward in forwards:
        forward.wait_recv()

    scale = head_size ** (-0.5) * 1.4426950408889634
    places = [(0, rows, HALO), (rows - HALO, HALO, 0), (0, HALO, rows + HALO)]

    def back(kind, h, offset):
        dest = (me + offset) % n_seq
        block = (dest + n_seq - (0, 1, n_seq - 1)[kind]) % n_seq
        first, size, at = places[kind]
        src = attended.at[h, pl.ds(pl.multiple_of(block * rows + first, HALO), size)]
        dst = parts.at[me, h, pl.ds(at, size)]
        row = kind * n_heads + h
        remote = pltpu.make_async_remote_copy(
            src_ref=src, dst_ref=dst, send_sem=back_send.at[row, offset], recv_sem=back_recv.at[row, offset],
            device_id=(dest, dp), device_id_type=MESH,
        )
        return remote, pltpu.make_async_copy(src, dst, back_recv.at[row, offset])

    for c in range(count):
        @pl.when(target != dp)
        def _():
            weights(c).wait()

        @pl.when(target == dp)
        def _():
            kept(c).wait()

        def product(s, carry):
            where = pl.ds(pl.multiple_of(s * rows, rows), rows)
            qkv = jnp.dot(normed[s], w_got[c][...], preferred_element_type=jnp.float32).astype(jnp.bfloat16)
            extra = lax.broadcasted_iota(jnp.int32, (rows, wide - head_size), 1)
            row = s * rows + lax.broadcasted_iota(jnp.int32, (rows, wide - head_size), 0)
            first = extra == 0
            ones = jnp.where(first, 1.0, 0.0).astype(jnp.bfloat16)
            bias = jnp.where(first & (row >= length_ref[0]), -1e30, 0.0).astype(jnp.bfloat16)
            for i, (h, p) in enumerate(pieces[c]):
                one = qkv[:, i * head_size : (i + 1) * head_size]
                if p == 0:
                    queries[h, where, :] = jnp.concatenate([one, ones], axis=1)
                elif p == 1:
                    keys_t[h, :, where] = jnp.concatenate([one, bias], axis=1).T
                else:
                    values[h, where, :] = jnp.concatenate([one, ones], axis=1)
            return carry

        lax.fori_loop(0, n_seq, product, 0)
        ready = [h for h in range(n_heads) if (h, 0) in pieces[c]]

        def attend(i, carry):
            block = (me + 1 + i) % n_seq
            where = pl.ds(pl.multiple_of(block * rows, rows), rows)
            for h in ready:
                scores = jnp.dot(queries[h, where, :], keys_t[h], preferred_element_type=jnp.float32)
                top = jnp.max(scores, axis=-1, keepdims=True)
                weight = jnp.exp2((scores - top) * scale).astype(jnp.bfloat16)
                summed = jnp.dot(weight, values[h], preferred_element_type=jnp.float32)
                attended[h, where, :] = (
                    summed[:, :head_size] / summed[:, head_size : head_size + 1]
                ).astype(jnp.bfloat16)
                for kind, shift in enumerate((0, 1, n_seq - 1)):
                    offset = (i + 1 + shift) % n_seq

                    @pl.when(offset != 0)
                    def _():
                        back(kind, h, offset)[0].start()

                    @pl.when(offset == 0)
                    def _():
                        back(kind, h, offset)[1].start()

            return carry

        lax.fori_loop(0, n_seq, attend, 0)

    for h in range(n_heads):
        for kind in range(3):
            back(kind, h, 0)[1].wait()
            for offset in range(1, n_seq):
                back(kind, h, offset)[0].wait()
    for reorder in reorders:
        reorder.wait()
    for copy in copies + forwards:
        copy.wait_send()
    finish(n_seq, length_ref, parts, frames, halo_out, wo_out, gain_conv, conv_w, out, mid, padded, heads)


def attention(length, frames, gain, gain_conv, conv_w, w, wo, n_seq, n_dp, head_size):
    rows, width = frames.shape
    total = n_seq * rows
    n_heads = w.shape[1] // (n_seq // n_dp) // (3 * head_size)
    half = n_seq // 2
    dma = pltpu.SemaphoreType.DMA
    if n_heads == 2:
        pieces = (((0, 0), (0, 1), (0, 2), (1, 1)), ((1, 0), (1, 2)))
    else:
        pieces = (tuple((h, p) for h in range(n_heads) for p in range(3)),)
    count = len(pieces)
    return pl.pallas_call(
        functools.partial(attention_kernel, n_seq, n_dp, head_size, pieces),
        out_shape=jax.ShapeDtypeStruct((rows, width), jnp.bfloat16),
        in_specs=[
            pl.BlockSpec(memory_space=pltpu.SMEM),
            pl.BlockSpec(memory_space=pltpu.HBM),
            pl.BlockSpec(memory_space=pltpu.VMEM),
            pl.BlockSpec(memory_space=pltpu.VMEM),
            pl.BlockSpec(memory_space=pltpu.VMEM),
            pl.BlockSpec(memory_space=pltpu.HBM),
            pl.BlockSpec(memory_space=pltpu.HBM),
        ],
        out_specs=pl.BlockSpec(memory_space=pltpu.VMEM),
        scratch_shapes=[
            pltpu.VMEM((n_seq, n_heads, rows + 2 * HALO, head_size), jnp.bfloat16),
            pltpu.VMEM((2, HALO, width), jnp.bfloat16),
            pltpu.VMEM(wo.shape, jnp.bfloat16),
            pltpu.VMEM((rows + 2 * HALO, width), jnp.float32),
            pltpu.VMEM((rows + 2 * HALO, width), jnp.float32),
            pltpu.VMEM((rows + 2 * HALO, width), jnp.bfloat16),
            pltpu.VMEM((rows, width), jnp.bfloat16),
            pltpu.VMEM((n_seq, rows, width), jnp.bfloat16),
            pltpu.VMEM(w.shape, jnp.bfloat16),
            pltpu.VMEM((n_heads, 128, total), jnp.bfloat16),
            pltpu.VMEM((n_heads, total, 128), jnp.bfloat16),
            pltpu.VMEM((n_heads, total, 128), jnp.bfloat16),
            pltpu.VMEM((n_heads, total, head_size), jnp.bfloat16),
            dma, dma, dma((n_seq,)), dma((count,)), dma((count,)), dma((2,)), dma((2,)),
            dma((half,)), dma((half,)), dma((half,)), dma((half,)),
            dma((3 * n_heads, n_seq)), dma((3 * n_heads, n_seq)),
        ]
        + [pltpu.VMEM((width, len(piece) * head_size), jnp.bfloat16) for piece in pieces] * 2,
        compiler_params=pltpu.CompilerParams(
            collective_id=0, has_side_effects=True, vmem_limit_bytes=58 * 1024 * 1024
        ),
    )(length, frames, gain, gain_conv, conv_w, w, wo)


def finish(n_seq, length_ref, parts, frames, halo, wo, gain, conv_w, out, mid, padded, heads):
    me = lax.axis_index("seq")
    count, width = frames.shape
    tall = count + 2 * HALO
    taps = conv_w.shape[0]
    reach = (taps - 1) // 2
    cut = 512
    heads[...] = jnp.concatenate(
        [parts[s, h] for s in range(n_seq) for h in range(parts.shape[1])], axis=1
    )
    for c in range(width // cut):
        columns = slice(c * cut, (c + 1) * cut)
        rows = jnp.concatenate([halo[0, :, columns], frames[:, columns], halo[1, :, columns]], axis=0)
        mid[:, columns] = rows.astype(jnp.float32) + jnp.dot(
            heads[...], wo[:, columns], preferred_element_type=jnp.float32
        )

    part = 96

    def norm_part(i, carry):
        start = pl.multiple_of(i * part, part)
        where = pl.ds(start, part)
        values = mid[where, :]
        mean = jnp.mean(values, axis=-1, keepdims=True)
        centred = values - mean
        var = jnp.mean(centred * centred, axis=-1, keepdims=True)
        position = me * count - HALO + start + lax.broadcasted_iota(jnp.int32, (part, 1), 0)
        valid = (position >= 0) & (position < length_ref[0])
        normed = centred * lax.rsqrt(var + 1e-05) * gain[...]
        padded[where, :] = jnp.where(valid, normed, 0.0).astype(jnp.bfloat16).astype(jnp.float32)
        return carry

    lax.fori_loop(0, tall // part, norm_part, 0)

    lanes = 128

    def conv_part(c, carry):
        columns = pl.ds(pl.multiple_of(c * lanes, lanes), lanes)
        for half in range(count // 128):
            base = half * 128
            conv = jnp.zeros((128, lanes), jnp.float32)
            for turn in range(8):
                group = [tap for tap in range(taps) if (tap + HALO - reach) % 8 == turn]
                if not group:
                    continue
                low = (group[0] + HALO - reach) // 8 * 8
                high = (group[-1] + HALO - reach) // 8 * 8
                moved = padded[base + low + turn : base + high + turn + 128, columns]
                for tap in group:
                    first = (tap + HALO - reach) // 8 * 8 - low
                    conv = conv + conv_w[tap : tap + 1, columns] * moved[first : first + 128]
            result = mid[base + HALO : base + HALO + 128, columns] + conv * jax.nn.sigmoid(conv)
            out[base : base + 128, columns] = result.astype(jnp.bfloat16)
        return carry

    lax.fori_loop(0, width // lanes, conv_part, 0)


def body(n_seq, n_dp, frames, lengths, wqkv, wo, gain_attn, gain_conv, conv_w):
    rows = frames[0]
    count, width = rows.shape
    head_size = width // HEADS
    return attention(
        lengths, rows, gain_attn[None], gain_conv[None], conv_w, wqkv, wo, n_seq, n_dp, head_size
    )[None]


def solution(mesh):
    return jax.shard_map(
        functools.partial(body, mesh.shape["seq"], mesh.shape["dp"]),
        mesh=mesh,
        in_specs=(P("dp", "seq", None), P("dp"), P(None, "dp"), P(), P(), P(), P()),
        out_specs=P("dp", "seq", None),
        check_vma=False,
    )
```

```python
import functools

import jax
import jax.numpy as jnp
from jax import lax
from jax.experimental import pallas as pl
from jax.experimental.pallas import tpu as pltpu
from jax.sharding import PartitionSpec as P

HEADS = 16
HALO = 16
MESH = pl.DeviceIdType.MESH


def reversed_bits(value, count):
    bits = count.bit_length() - 1
    out = 0
    for i in range(bits):
        out = out + (value // (1 << i)) % 2 * (1 << (bits - 1 - i))
    return out


def head_group(seq, dp, n_seq, n_dp):
    column = seq // (n_seq // n_dp)
    return (reversed_bits(dp, n_dp) + column) % n_dp


def attention_kernel(
    n_seq, n_dp, head_size, pieces, length_ref, frames_ref, gain, gain_conv, conv_w, w_ref, wo_ref, out,
    parts, halo_out, wo_out, mid, padded, heads,
    frames, normed, w_full, keys_t, values, queries, attended,
    frame_sem, w_sem, wo_sem, w_send, w_recv, halo_send, halo_recv,
    send_sem, recv_sem, forward_send, forward_recv, back_send, back_recv, *w_parts,
):
    count = len(pieces)
    w_own, w_got = w_parts[:count], w_parts[count:]
    me = lax.axis_index("seq")
    dp = lax.axis_index("dp")
    rows, width = frames.shape
    total = n_seq * rows
    half = n_seq // 2
    column = me // (n_seq // n_dp)
    source = head_group(me, dp, n_seq, n_dp)
    target = reversed_bits((dp + n_dp - column) % n_dp, n_dp)
    sibling = me + 1 - 2 * (me % 2)
    left = (me + n_seq - 1) % n_seq
    right = (me + 1) % n_seq
    peers = [(me + 2 * i) % n_seq for i in range(1, half)]
    n_heads = attended.shape[0]
    share = n_seq // n_dp
    wide = 128

    w_load = pltpu.make_async_copy(w_ref, w_full, w_sem)
    w_load.start()
    load = pltpu.make_async_copy(frames_ref, frames, frame_sem)
    load.start()
    barrier = pltpu.get_barrier_semaphore()
    for i in range(1, n_seq):
        pl.semaphore_signal(barrier, inc=1, device_id=((me + i) % n_seq, dp), device_id_type=MESH)

    @pl.when(target != dp)
    def _():
        pl.semaphore_signal(barrier, inc=1, device_id=(me, source), device_id_type=MESH)
        pl.semaphore_signal(barrier, inc=1, device_id=(me, target), device_id_type=MESH)
        pl.semaphore_wait(barrier, n_seq + 1)

    @pl.when(target == dp)
    def _():
        pl.semaphore_wait(barrier, n_seq - 1)

    def weights(c):
        return pltpu.make_async_remote_copy(
            src_ref=w_own[c], dst_ref=w_got[c], send_sem=w_send.at[c], recv_sem=w_recv.at[c],
            device_id=(me, target), device_id_type=MESH,
        )

    def kept(c):
        return pltpu.make_async_copy(w_own[c], w_got[c], w_recv.at[c])

    w_load.wait()
    for c in range(count):
        for j in range(share):
            @pl.when(me % share == j)
            def _():
                def cut(i, carry):
                    where = pl.ds(pl.multiple_of(i * 256, 256), 256)
                    w_own[c][where, :] = jnp.concatenate(
                        [
                            w_full[where, ((j * n_heads + h) * 3 + p) * head_size : ((j * n_heads + h) * 3 + p + 1) * head_size]
                            for h, p in pieces[c]
                        ],
                        axis=1,
                    )
                    return carry

                lax.fori_loop(0, width // 256, cut, 0)

        if c == 0:
            @pl.when(target != dp)
            def _():
                weights(c).start()

        @pl.when(target == dp)
        def _():
            kept(c).start()

    load.wait()
    part = 64

    def norm_part(i, carry):
        where = pl.ds(pl.multiple_of(i * part, part), part)
        numbers = frames[where, :].astype(jnp.float32)
        mean = jnp.mean(numbers, axis=-1, keepdims=True)
        centred = numbers - mean
        var = jnp.mean(centred * centred, axis=-1, keepdims=True)
        normed[me, where, :] = (centred * lax.rsqrt(var + 1e-05) * gain[...][None, :]).astype(jnp.bfloat16)
        return carry

    lax.fori_loop(0, rows // part, norm_part, 0)

    copies = []
    for i in range(half):
        copies.append(pltpu.make_async_remote_copy(
            src_ref=normed.at[me], dst_ref=normed.at[me], send_sem=send_sem.at[i], recv_sem=recv_sem.at[i],
            device_id=(peers[i - 1] if i else sibling, dp), device_id_type=MESH,
        ))
    copies.append(pltpu.make_async_remote_copy(
        src_ref=frames.at[pl.ds(0, HALO)], dst_ref=halo_out.at[1],
        send_sem=halo_send.at[0], recv_sem=halo_recv.at[0],
        device_id=(left, dp), device_id_type=MESH,
    ))
    copies.append(pltpu.make_async_remote_copy(
        src_ref=frames.at[pl.ds(rows - HALO, HALO)], dst_ref=halo_out.at[0],
        send_sem=halo_send.at[1], recv_sem=halo_recv.at[1],
        device_id=(right, dp), device_id_type=MESH,
    ))
    for copy in copies[1:] + copies[:1]:
        copy.start()

    depth = n_heads * head_size
    reorders = []
    for i in range(n_seq):
        slot = head_group(i, dp, n_seq, n_dp) * share + i % share
        reorder = pltpu.make_async_copy(
            wo_ref.at[pl.ds(pl.multiple_of(slot * depth, depth), depth)],
            wo_out.at[pl.ds(i * depth, depth)],
            wo_sem.at[i],
        )
        reorder.start()
        reorders.append(reorder)

    forwards = []
    for i in range(1, half):
        origin = (me + n_seq - 2 * i) % n_seq
        copies[i].wait_recv()
        forward = pltpu.make_async_remote_copy(
            src_ref=normed.at[origin], dst_ref=normed.at[origin],
            send_sem=forward_send.at[i], recv_sem=forward_recv.at[i],
            device_id=(sibling, dp), device_id_type=MESH,
        )
        forward.start()
        forwards.append(forward)
        if i == 1:
            @pl.when(target != dp)
            def _():
                for c in range(1, count):
                    weights(c - 1).wait_send()
                    weights(c).start()
    for copy in copies[:1] + copies[half:]:
        copy.wait_recv()
    for forward in forwards:
        forward.wait_recv()

    scale = head_size ** (-0.5) * 1.4426950408889634
    places = [(0, rows, HALO), (rows - HALO, HALO, 0), (0, HALO, rows + HALO)]

    def back(kind, h, offset):
        dest = (me + offset) % n_seq
        block = (dest + n_seq - (0, 1, n_seq - 1)[kind]) % n_seq
        first, size, at = places[kind]
        src = attended.at[h, pl.ds(pl.multiple_of(block * rows + first, HALO), size)]
        dst = parts.at[me, h, pl.ds(at, size)]
        row = kind * n_heads + h
        remote = pltpu.make_async_remote_copy(
            src_ref=src, dst_ref=dst, send_sem=back_send.at[row, offset], recv_sem=back_recv.at[row, offset],
            device_id=(dest, dp), device_id_type=MESH,
        )
        return remote, pltpu.make_async_copy(src, dst, back_recv.at[row, offset])

    for c in range(count):
        @pl.when(target != dp)
        def _():
            weights(c).wait_recv()
            if c == count - 1:
                weights(c).wait_send()

        @pl.when(target == dp)
        def _():
            kept(c).wait()

        def product(s, carry):
            where = pl.ds(pl.multiple_of(s * rows, rows), rows)
            qkv = jnp.dot(normed[s], w_got[c][...], preferred_element_type=jnp.float32).astype(jnp.bfloat16)
            extra = lax.broadcasted_iota(jnp.int32, (rows, wide - head_size), 1)
            row = s * rows + lax.broadcasted_iota(jnp.int32, (rows, wide - head_size), 0)
            first = extra == 0
            ones = jnp.where(first, 1.0, 0.0).astype(jnp.bfloat16)
            bias = jnp.where(first & (row >= length_ref[0]), -1e30, 0.0).astype(jnp.bfloat16)
            for i, (h, p) in enumerate(pieces[c]):
                one = qkv[:, i * head_size : (i + 1) * head_size]
                if p == 0:
                    queries[h, where, :] = jnp.concatenate([one, ones], axis=1)
                elif p == 1:
                    keys_t[h, :, where] = jnp.concatenate([one, bias], axis=1).T
                else:
                    values[h, where, :] = jnp.concatenate([one, ones], axis=1)
            return carry

        lax.fori_loop(0, n_seq, product, 0)
        ready = [h for h in range(n_heads) if (h, 0) in pieces[c]]

        def attend(pair, carry):
            for h in ready:
                for i in (2 * pair, 2 * pair + 1):
                    block = (me + 1 + i) % n_seq
                    where = pl.ds(pl.multiple_of(block * rows, rows), rows)
                    scores = jnp.dot(queries[h, where, :], keys_t[h], preferred_element_type=jnp.float32)
                    top = jnp.max(scores, axis=-1, keepdims=True)
                    weight = jnp.exp2((scores - top) * scale).astype(jnp.bfloat16)
                    summed = jnp.dot(weight, values[h], preferred_element_type=jnp.float32)
                    attended[h, where, :] = (
                        summed[:, :head_size] / summed[:, head_size : head_size + 1]
                    ).astype(jnp.bfloat16)
            for h in ready:
                for i in (2 * pair, 2 * pair + 1):
                    for kind, shift in enumerate((0, 1, n_seq - 1)):
                        offset = (i + 1 + shift) % n_seq

                        @pl.when(offset != 0)
                        def _():
                            back(kind, h, offset)[0].start()

                        @pl.when(offset == 0)
                        def _():
                            back(kind, h, offset)[1].start()

            return carry

        lax.fori_loop(0, n_seq // 2, attend, 0)

    for h in range(n_heads):
        for kind in range(3):
            back(kind, h, 0)[1].wait()
            for offset in range(1, n_seq):
                back(kind, h, offset)[0].wait()
    for reorder in reorders:
        reorder.wait()
    for copy in copies + forwards:
        copy.wait_send()
    finish(n_seq, length_ref, parts, frames, halo_out, wo_out, gain_conv, conv_w, out, mid, padded, heads)


def attention(length, frames, gain, gain_conv, conv_w, w, wo, n_seq, n_dp, head_size):
    rows, width = frames.shape
    total = n_seq * rows
    n_heads = w.shape[1] // (n_seq // n_dp) // (3 * head_size)
    half = n_seq // 2
    dma = pltpu.SemaphoreType.DMA
    if n_heads == 2:
        pieces = (((0, 0), (0, 1), (0, 2), (1, 1)), ((1, 0), (1, 2)))
    else:
        pieces = (tuple((h, p) for h in range(n_heads) for p in range(3)),)
    count = len(pieces)
    return pl.pallas_call(
        functools.partial(attention_kernel, n_seq, n_dp, head_size, pieces),
        out_shape=jax.ShapeDtypeStruct((rows, width), jnp.bfloat16),
        in_specs=[
            pl.BlockSpec(memory_space=pltpu.SMEM),
            pl.BlockSpec(memory_space=pltpu.HBM),
            pl.BlockSpec(memory_space=pltpu.VMEM),
            pl.BlockSpec(memory_space=pltpu.VMEM),
            pl.BlockSpec(memory_space=pltpu.VMEM),
            pl.BlockSpec(memory_space=pltpu.HBM),
            pl.BlockSpec(memory_space=pltpu.HBM),
        ],
        out_specs=pl.BlockSpec(memory_space=pltpu.VMEM),
        scratch_shapes=[
            pltpu.VMEM((n_seq, n_heads, rows + 2 * HALO, head_size), jnp.bfloat16),
            pltpu.VMEM((2, HALO, width), jnp.bfloat16),
            pltpu.VMEM(wo.shape, jnp.bfloat16),
            pltpu.VMEM((rows + 2 * HALO, width), jnp.float32),
            pltpu.VMEM((rows + 2 * HALO, width), jnp.float32),
            pltpu.VMEM((rows + 2 * HALO, width), jnp.bfloat16),
            pltpu.VMEM((rows, width), jnp.bfloat16),
            pltpu.VMEM((n_seq, rows, width), jnp.bfloat16),
            pltpu.VMEM(w.shape, jnp.bfloat16),
            pltpu.VMEM((n_heads, 128, total), jnp.bfloat16),
            pltpu.VMEM((n_heads, total, 128), jnp.bfloat16),
            pltpu.VMEM((n_heads, total, 128), jnp.bfloat16),
            pltpu.VMEM((n_heads, total, head_size), jnp.bfloat16),
            dma, dma, dma((n_seq,)), dma((count,)), dma((count,)), dma((2,)), dma((2,)),
            dma((half,)), dma((half,)), dma((half,)), dma((half,)),
            dma((3 * n_heads, n_seq)), dma((3 * n_heads, n_seq)),
        ]
        + [pltpu.VMEM((width, len(piece) * head_size), jnp.bfloat16) for piece in pieces] * 2,
        compiler_params=pltpu.CompilerParams(
            collective_id=0, has_side_effects=True, vmem_limit_bytes=58 * 1024 * 1024
        ),
    )(length, frames, gain, gain_conv, conv_w, w, wo)


def finish(n_seq, length_ref, parts, frames, halo, wo, gain, conv_w, out, mid, padded, heads):
    me = lax.axis_index("seq")
    count, width = frames.shape
    tall = count + 2 * HALO
    taps = conv_w.shape[0]
    reach = (taps - 1) // 2
    cut = 512
    heads[...] = jnp.concatenate(
        [parts[s, h] for s in range(n_seq) for h in range(parts.shape[1])], axis=1
    )
    for c in range(width // cut):
        columns = slice(c * cut, (c + 1) * cut)
        rows = jnp.concatenate([halo[0, :, columns], frames[:, columns], halo[1, :, columns]], axis=0)
        mid[:, columns] = rows.astype(jnp.float32) + jnp.dot(
            heads[...], wo[:, columns], preferred_element_type=jnp.float32
        )

    part = 96

    def norm_part(i, carry):
        start = pl.multiple_of(i * part, part)
        where = pl.ds(start, part)
        values = mid[where, :]
        mean = jnp.mean(values, axis=-1, keepdims=True)
        centred = values - mean
        var = jnp.mean(centred * centred, axis=-1, keepdims=True)
        position = me * count - HALO + start + lax.broadcasted_iota(jnp.int32, (part, 1), 0)
        valid = (position >= 0) & (position < length_ref[0])
        normed = centred * lax.rsqrt(var + 1e-05) * gain[...][None, :]
        padded[where, :] = jnp.where(valid, normed, 0.0).astype(jnp.bfloat16).astype(jnp.float32)
        return carry

    lax.fori_loop(0, tall // part, norm_part, 0)

    lanes = 128

    def conv_part(c, carry):
        columns = pl.ds(pl.multiple_of(c * lanes, lanes), lanes)
        for half in range(count // 128):
            base = half * 128
            conv = jnp.zeros((128, lanes), jnp.float32)
            for turn in range(8):
                group = [tap for tap in range(taps) if (tap + HALO - reach) % 8 == turn]
                if not group:
                    continue
                low = (group[0] + HALO - reach) // 8 * 8
                high = (group[-1] + HALO - reach) // 8 * 8
                moved = padded[base + low + turn : base + high + turn + 128, columns]
                for tap in group:
                    first = (tap + HALO - reach) // 8 * 8 - low
                    conv = conv + conv_w[tap : tap + 1, columns] * moved[first : first + 128]
            result = mid[base + HALO : base + HALO + 128, columns] + conv * jax.nn.sigmoid(conv)
            out[base : base + 128, columns] = result.astype(jnp.bfloat16)
        return carry

    lax.fori_loop(0, width // lanes, conv_part, 0)


def body(n_seq, n_dp, frames, lengths, wqkv, wo, gain_attn, gain_conv, conv_w):
    rows = frames[0]
    count, width = rows.shape
    head_size = width // HEADS
    return attention(
        lengths, rows, gain_attn, gain_conv, conv_w, wqkv, wo, n_seq, n_dp, head_size
    )[None]


def solution(mesh):
    return jax.shard_map(
        functools.partial(body, mesh.shape["seq"], mesh.shape["dp"]),
        mesh=mesh,
        in_specs=(P("dp", "seq", None), P("dp"), P(None, "dp"), P(), P(), P(), P()),
        out_specs=P("dp", "seq", None),
        check_vma=False,
    )
```

```python
import functools

import jax
import jax.numpy as jnp
from jax import lax
from jax.experimental import pallas as pl
from jax.experimental.pallas import tpu as pltpu
from jax.sharding import PartitionSpec as P

HEADS = 16
HALO = 16
MESH = pl.DeviceIdType.MESH


def reversed_bits(value, count):
    bits = count.bit_length() - 1
    out = 0
    for i in range(bits):
        out = out + (value // (1 << i)) % 2 * (1 << (bits - 1 - i))
    return out


def head_group(seq, dp, n_seq, n_dp):
    column = seq // (n_seq // n_dp)
    return (reversed_bits(dp, n_dp) + column) % n_dp


def attention_kernel(
    n_seq, n_dp, head_size, pieces, length_ref, frames_ref, gain, gain_conv, conv_w, w_ref, wo_ref, out,
    parts, halo_out, wo_out, mid, padded, heads,
    frames, normed, w_full, keys_t, values, queries, attended,
    frame_sem, w_sem, wo_sem, w_send, w_recv, halo_send, halo_recv,
    send_sem, recv_sem, forward_send, forward_recv, back_send, back_recv, *w_parts,
):
    count = len(pieces)
    w_own, w_got = w_parts[:count], w_parts[count:]
    me = lax.axis_index("seq")
    dp = lax.axis_index("dp")
    rows, width = frames.shape
    total = n_seq * rows
    half = n_seq // 2
    column = me // (n_seq // n_dp)
    source = head_group(me, dp, n_seq, n_dp)
    target = reversed_bits((dp + n_dp - column) % n_dp, n_dp)
    sibling = me + 1 - 2 * (me % 2)
    left = (me + n_seq - 1) % n_seq
    right = (me + 1) % n_seq
    peers = [(me + 2 * i) % n_seq for i in range(1, half)]
    n_heads = attended.shape[0]
    share = n_seq // n_dp
    wide = 128

    w_load = pltpu.make_async_copy(w_ref, w_full, w_sem)
    w_load.start()
    load = pltpu.make_async_copy(frames_ref, frames, frame_sem)
    load.start()
    barrier = pltpu.get_barrier_semaphore()
    for i in range(1, n_seq):
        pl.semaphore_signal(barrier, inc=1, device_id=((me + i) % n_seq, dp), device_id_type=MESH)

    @pl.when(target != dp)
    def _():
        pl.semaphore_signal(barrier, inc=1, device_id=(me, source), device_id_type=MESH)
        pl.semaphore_signal(barrier, inc=1, device_id=(me, target), device_id_type=MESH)
        pl.semaphore_wait(barrier, n_seq + 1)

    @pl.when(target == dp)
    def _():
        pl.semaphore_wait(barrier, n_seq - 1)

    def weights(c):
        return pltpu.make_async_remote_copy(
            src_ref=w_own[c], dst_ref=w_got[c], send_sem=w_send.at[c], recv_sem=w_recv.at[c],
            device_id=(me, target), device_id_type=MESH,
        )

    def kept(c):
        return pltpu.make_async_copy(w_own[c], w_got[c], w_recv.at[c])

    load.wait()
    part = 64

    def norm_part(i, carry):
        where = pl.ds(pl.multiple_of(i * part, part), part)
        numbers = frames[where, :].astype(jnp.float32)
        mean = jnp.mean(numbers, axis=-1, keepdims=True)
        centred = numbers - mean
        var = jnp.mean(centred * centred, axis=-1, keepdims=True)
        normed[me, where, :] = (centred * lax.rsqrt(var + 1e-05) * gain[...][None, :]).astype(jnp.bfloat16)
        return carry

    lax.fori_loop(0, rows // part, norm_part, 0)

    copies = []
    for i in range(half):
        copies.append(pltpu.make_async_remote_copy(
            src_ref=normed.at[me], dst_ref=normed.at[me], send_sem=send_sem.at[i], recv_sem=recv_sem.at[i],
            device_id=(peers[i - 1] if i else sibling, dp), device_id_type=MESH,
        ))
    copies.append(pltpu.make_async_remote_copy(
        src_ref=frames.at[pl.ds(0, HALO)], dst_ref=halo_out.at[1],
        send_sem=halo_send.at[0], recv_sem=halo_recv.at[0],
        device_id=(left, dp), device_id_type=MESH,
    ))
    copies.append(pltpu.make_async_remote_copy(
        src_ref=frames.at[pl.ds(rows - HALO, HALO)], dst_ref=halo_out.at[0],
        send_sem=halo_send.at[1], recv_sem=halo_recv.at[1],
        device_id=(right, dp), device_id_type=MESH,
    ))
    for copy in copies[1:] + copies[:1]:
        copy.start()

    w_load.wait()
    for c in range(count):
        for j in range(share):
            @pl.when(me % share == j)
            def _():
                def cut(i, carry):
                    where = pl.ds(pl.multiple_of(i * 256, 256), 256)
                    w_own[c][where, :] = jnp.concatenate(
                        [
                            w_full[where, ((j * n_heads + h) * 3 + p) * head_size : ((j * n_heads + h) * 3 + p + 1) * head_size]
                            for h, p in pieces[c]
                        ],
                        axis=1,
                    )
                    return carry

                lax.fori_loop(0, width // 256, cut, 0)

        if c == 0:
            @pl.when(target != dp)
            def _():
                weights(c).start()

        @pl.when(target == dp)
        def _():
            kept(c).start()

    depth = n_heads * head_size
    reorders = []
    for i in range(n_seq):
        slot = head_group(i, dp, n_seq, n_dp) * share + i % share
        reorder = pltpu.make_async_copy(
            wo_ref.at[pl.ds(pl.multiple_of(slot * depth, depth), depth)],
            wo_out.at[pl.ds(i * depth, depth)],
            wo_sem.at[i],
        )
        reorder.start()
        reorders.append(reorder)

    forwards = []
    for i in range(1, half):
        origin = (me + n_seq - 2 * i) % n_seq
        copies[i].wait_recv()
        forward = pltpu.make_async_remote_copy(
            src_ref=normed.at[origin], dst_ref=normed.at[origin],
            send_sem=forward_send.at[i], recv_sem=forward_recv.at[i],
            device_id=(sibling, dp), device_id_type=MESH,
        )
        forward.start()
        forwards.append(forward)
        if i == 1:
            @pl.when(target != dp)
            def _():
                for c in range(1, count):
                    weights(c - 1).wait_send()
                    weights(c).start()
    for copy in copies[:1] + copies[half:]:
        copy.wait_recv()
    for forward in forwards:
        forward.wait_recv()

    scale = head_size ** (-0.5) * 1.4426950408889634
    places = [(0, rows, HALO), (rows - HALO, HALO, 0), (0, HALO, rows + HALO)]

    def back(kind, h, offset):
        dest = (me + offset) % n_seq
        block = (dest + n_seq - (0, 1, n_seq - 1)[kind]) % n_seq
        first, size, at = places[kind]
        src = attended.at[h, pl.ds(pl.multiple_of(block * rows + first, HALO), size)]
        dst = parts.at[me, h, pl.ds(at, size)]
        row = kind * n_heads + h
        remote = pltpu.make_async_remote_copy(
            src_ref=src, dst_ref=dst, send_sem=back_send.at[row, offset], recv_sem=back_recv.at[row, offset],
            device_id=(dest, dp), device_id_type=MESH,
        )
        return remote, pltpu.make_async_copy(src, dst, back_recv.at[row, offset])

    for c in range(count):
        @pl.when(target != dp)
        def _():
            weights(c).wait_recv()
            if c == count - 1:
                weights(c).wait_send()

        @pl.when(target == dp)
        def _():
            kept(c).wait()

        def product(s, carry):
            where = pl.ds(pl.multiple_of(s * rows, rows), rows)
            qkv = jnp.dot(normed[s], w_got[c][...], preferred_element_type=jnp.float32).astype(jnp.bfloat16)
            extra = lax.broadcasted_iota(jnp.int32, (rows, wide - head_size), 1)
            row = s * rows + lax.broadcasted_iota(jnp.int32, (rows, wide - head_size), 0)
            first = extra == 0
            ones = jnp.where(first, 1.0, 0.0).astype(jnp.bfloat16)
            bias = jnp.where(first & (row >= length_ref[0]), -1e30, 0.0).astype(jnp.bfloat16)
            for i, (h, p) in enumerate(pieces[c]):
                one = qkv[:, i * head_size : (i + 1) * head_size]
                if p == 0:
                    queries[h, where, :] = jnp.concatenate([one, ones], axis=1)
                elif p == 1:
                    keys_t[h, :, where] = jnp.concatenate([one, bias], axis=1).T
                else:
                    values[h, where, :] = jnp.concatenate([one, ones], axis=1)
            return carry

        lax.fori_loop(0, n_seq, product, 0)
        ready = [h for h in range(n_heads) if (h, 0) in pieces[c]]

        def attend(pair, carry):
            for h in ready:
                for i in (2 * pair, 2 * pair + 1):
                    block = (me + 1 + i) % n_seq
                    where = pl.ds(pl.multiple_of(block * rows, rows), rows)
                    scores = jnp.dot(queries[h, where, :], keys_t[h], preferred_element_type=jnp.float32)
                    top = jnp.max(scores, axis=-1, keepdims=True)
                    weight = jnp.exp2((scores - top) * scale).astype(jnp.bfloat16)
                    summed = jnp.dot(weight, values[h], preferred_element_type=jnp.float32)
                    attended[h, where, :] = (
                        summed[:, :head_size] / summed[:, head_size : head_size + 1]
                    ).astype(jnp.bfloat16)
            for h in ready:
                for i in (2 * pair, 2 * pair + 1):
                    for kind, shift in enumerate((0, 1, n_seq - 1)):
                        offset = (i + 1 + shift) % n_seq

                        @pl.when(offset != 0)
                        def _():
                            back(kind, h, offset)[0].start()

                        @pl.when(offset == 0)
                        def _():
                            back(kind, h, offset)[1].start()

            return carry

        lax.fori_loop(0, n_seq // 2, attend, 0)

    for h in range(n_heads):
        for kind in range(3):
            back(kind, h, 0)[1].wait()
            for offset in range(1, n_seq):
                back(kind, h, offset)[0].wait()
    for reorder in reorders:
        reorder.wait()
    for copy in copies + forwards:
        copy.wait_send()
    finish(n_seq, length_ref, parts, frames, halo_out, wo_out, gain_conv, conv_w, out, mid, padded, heads)


def attention(length, frames, gain, gain_conv, conv_w, w, wo, n_seq, n_dp, head_size):
    rows, width = frames.shape
    total = n_seq * rows
    n_heads = w.shape[1] // (n_seq // n_dp) // (3 * head_size)
    half = n_seq // 2
    dma = pltpu.SemaphoreType.DMA
    if n_heads == 2:
        pieces = (((0, 0), (0, 1), (0, 2), (1, 1)), ((1, 0), (1, 2)))
    else:
        pieces = (tuple((h, p) for h in range(n_heads) for p in range(3)),)
    count = len(pieces)
    return pl.pallas_call(
        functools.partial(attention_kernel, n_seq, n_dp, head_size, pieces),
        out_shape=jax.ShapeDtypeStruct((rows, width), jnp.bfloat16),
        in_specs=[
            pl.BlockSpec(memory_space=pltpu.SMEM),
            pl.BlockSpec(memory_space=pltpu.HBM),
            pl.BlockSpec(memory_space=pltpu.VMEM),
            pl.BlockSpec(memory_space=pltpu.VMEM),
            pl.BlockSpec(memory_space=pltpu.VMEM),
            pl.BlockSpec(memory_space=pltpu.HBM),
            pl.BlockSpec(memory_space=pltpu.HBM),
        ],
        out_specs=pl.BlockSpec(memory_space=pltpu.VMEM),
        scratch_shapes=[
            pltpu.VMEM((n_seq, n_heads, rows + 2 * HALO, head_size), jnp.bfloat16),
            pltpu.VMEM((2, HALO, width), jnp.bfloat16),
            pltpu.VMEM(wo.shape, jnp.bfloat16),
            pltpu.VMEM((rows + 2 * HALO, width), jnp.float32),
            pltpu.VMEM((rows + 2 * HALO, width), jnp.float32),
            pltpu.VMEM((rows + 2 * HALO, width), jnp.bfloat16),
            pltpu.VMEM((rows, width), jnp.bfloat16),
            pltpu.VMEM((n_seq, rows, width), jnp.bfloat16),
            pltpu.VMEM(w.shape, jnp.bfloat16),
            pltpu.VMEM((n_heads, 128, total), jnp.bfloat16),
            pltpu.VMEM((n_heads, total, 128), jnp.bfloat16),
            pltpu.VMEM((n_heads, total, 128), jnp.bfloat16),
            pltpu.VMEM((n_heads, total, head_size), jnp.bfloat16),
            dma, dma, dma((n_seq,)), dma((count,)), dma((count,)), dma((2,)), dma((2,)),
            dma((half,)), dma((half,)), dma((half,)), dma((half,)),
            dma((3 * n_heads, n_seq)), dma((3 * n_heads, n_seq)),
        ]
        + [pltpu.VMEM((width, len(piece) * head_size), jnp.bfloat16) for piece in pieces] * 2,
        compiler_params=pltpu.CompilerParams(
            collective_id=0, has_side_effects=True, vmem_limit_bytes=58 * 1024 * 1024
        ),
    )(length, frames, gain, gain_conv, conv_w, w, wo)


def finish(n_seq, length_ref, parts, frames, halo, wo, gain, conv_w, out, mid, padded, heads):
    me = lax.axis_index("seq")
    count, width = frames.shape
    tall = count + 2 * HALO
    taps = conv_w.shape[0]
    reach = (taps - 1) // 2
    cut = 512
    heads[...] = jnp.concatenate(
        [parts[s, h] for s in range(n_seq) for h in range(parts.shape[1])], axis=1
    )
    for c in range(width // cut):
        columns = slice(c * cut, (c + 1) * cut)
        rows = jnp.concatenate([halo[0, :, columns], frames[:, columns], halo[1, :, columns]], axis=0)
        mid[:, columns] = rows.astype(jnp.float32) + jnp.dot(
            heads[...], wo[:, columns], preferred_element_type=jnp.float32
        )

    part = 96

    def norm_part(i, carry):
        start = pl.multiple_of(i * part, part)
        where = pl.ds(start, part)
        values = mid[where, :]
        mean = jnp.mean(values, axis=-1, keepdims=True)
        centred = values - mean
        var = jnp.mean(centred * centred, axis=-1, keepdims=True)
        position = me * count - HALO + start + lax.broadcasted_iota(jnp.int32, (part, 1), 0)
        valid = (position >= 0) & (position < length_ref[0])
        normed = centred * lax.rsqrt(var + 1e-05) * gain[...][None, :]
        padded[where, :] = jnp.where(valid, normed, 0.0).astype(jnp.bfloat16).astype(jnp.float32)
        return carry

    lax.fori_loop(0, tall // part, norm_part, 0)

    lanes = 128

    def conv_part(c, carry):
        columns = pl.ds(pl.multiple_of(c * lanes, lanes), lanes)
        for half in range(count // 128):
            base = half * 128
            conv = jnp.zeros((128, lanes), jnp.float32)
            for turn in range(8):
                group = [tap for tap in range(taps) if (tap + HALO - reach) % 8 == turn]
                if not group:
                    continue
                low = (group[0] + HALO - reach) // 8 * 8
                high = (group[-1] + HALO - reach) // 8 * 8
                moved = padded[base + low + turn : base + high + turn + 128, columns]
                for tap in group:
                    first = (tap + HALO - reach) // 8 * 8 - low
                    conv = conv + conv_w[tap : tap + 1, columns] * moved[first : first + 128]
            result = mid[base + HALO : base + HALO + 128, columns] + conv * jax.nn.sigmoid(conv)
            out[base : base + 128, columns] = result.astype(jnp.bfloat16)
        return carry

    lax.fori_loop(0, width // lanes, conv_part, 0)


def body(n_seq, n_dp, frames, lengths, wqkv, wo, gain_attn, gain_conv, conv_w):
    rows = frames[0]
    count, width = rows.shape
    head_size = width // HEADS
    return attention(
        lengths, rows, gain_attn, gain_conv, conv_w, wqkv, wo, n_seq, n_dp, head_size
    )[None]


def solution(mesh):
    return jax.shard_map(
        functools.partial(body, mesh.shape["seq"], mesh.shape["dp"]),
        mesh=mesh,
        in_specs=(P("dp", "seq", None), P("dp"), P(None, "dp"), P(), P(), P(), P()),
        out_specs=P("dp", "seq", None),
        check_vma=False,
    )
```
